32 devices in a mesh: leaf: 32 (over z, y, x, core).
Axes of the slice: x: 2, y: 2, z: 4, core: 2. Of those that a mesh axis runs over, the one named last changes fastest.
Arguments:
- right_side: bfloat16 [32768, 256], P('leaf'), may hold values from -6 to 6
- leaf_inv: bfloat16 [32768, 1024], P('leaf'), may hold values from -0.1875 to 0.1875
- right_basis: bfloat16 [4, 32768, 256], P(None, 'leaf'), may hold values from -0.0625 to 0.0625
- left_basis: bfloat16 [4, 32768, 256], P(None, 'leaf'), may hold values from -0.375 to 0.375
- reduced_first: float32 [512, 512], P('leaf'), may hold values from -0.25 to 0.25
- reduced_second: float32 [1024, 512], P('leaf'), may hold values from -0.25 to 0.25
- reduced_third: float32 [2048, 512], P('leaf'), may hold values from -0.25 to 0.25
- reduced_fourth: float32 [4096, 512], P('leaf'), may hold values from -0.25 to 0.25
Outputs:
- solution: float32 [32768, 256], P('leaf')
The draws below stay inside these ranges and needn't reach their ends.
All inputs are finite; a program needn't handle non-finite values.
Results may differ from the reference program's by a relative error of at most 0.0003.
Values sent between devices are 32-bit elements; how exact they have to be, the bound alone decides.
A program may use at most 64 MiB of HBM per device.

```python
import jax
import jax.numpy as jnp
from jax import lax

LEAF = 1024
COLS = 256
RANK = 256
LEVELS = 4
UNKNOWNS = 32768
N_LEAF = 32


def shard_levels(own_key, extent, split, least, top_value):
    def one(position, blocks):
        draws = jax.random.uniform(jax.random.fold_in(jax.random.fold_in(own_key, 6), position), (blocks,), jnp.float32, least / len(split), top_value / len(split))
        return jnp.repeat(jnp.exp(draws), extent[position] // blocks).reshape((-1,) + (1,) * (len(extent) - position - 1))

    loudness = one(*split[0])
    for cut in split[1:]:
        loudness = loudness * one(*cut)
    return loudness


def noise(stream_key, extent, deviation, limit, cuts=(), kind=jnp.bfloat16):
    gain = shard_levels(stream_key, extent, cuts, -0.22, 0.18) if cuts else 1.0
    result = jax.random.normal(stream_key, extent, jnp.float32) * deviation * gain
    return jnp.minimum(jnp.maximum(result, -limit), limit).astype(kind)


def setup_inputs(seed: int = 0) -> dict:
    key_of = jax.random.split(jax.random.key(seed), 9)
    return {
        "right_side": noise(key_of[0], (UNKNOWNS, COLS), 1.0, 6.0, ((0, 32),)),
        "leaf_inv": noise(key_of[1], (UNKNOWNS, LEAF), LEAF ** -0.5, 0.1875, ((0, 32),)),
        "right_basis": noise(key_of[2], (LEVELS, UNKNOWNS, RANK), (LEAF * N_LEAF // 4) ** -0.5, 0.0625, ((1, 32),)),
        "left_basis": noise(key_of[3], (LEVELS, UNKNOWNS, RANK), RANK ** -0.5, 0.375, ((1, 32),)),
        "reduced_first": noise(key_of[4], (RANK * 2, 2 * RANK), (2 * RANK) ** -0.5, 0.25, ((0, 32),), jnp.float32),
        "reduced_second": noise(key_of[5], (RANK * 4, 2 * RANK), (2 * RANK) ** -0.5, 0.25, ((0, 32),), jnp.float32),
        "reduced_third": noise(key_of[6], (RANK * 8, 2 * RANK), (2 * RANK) ** -0.5, 0.25, ((0, 32),), jnp.float32),
        "reduced_fourth": noise(key_of[7], (RANK * 16, 2 * RANK), (2 * RANK) ** -0.5, 0.25, ((0, 32),), jnp.float32),
    }


def leaf_apply(pair):
    return jnp.dot(pair[0], pair[1], preferred_element_type=jnp.float32)


def reference(right_side, leaf_inv, right_basis, left_basis, reduced_first, reduced_second, reduced_third, reduced_fourth):
    devices_all = N_LEAF
    blocks = right_side.reshape(devices_all, LEAF, COLS)
    inverses = leaf_inv.reshape(devices_all, LEAF, LEAF)
    solution = lax.map(leaf_apply, (inverses, blocks))
    reduced_all = (reduced_first, reduced_second, reduced_third, reduced_fourth)
    for level in range(LEVELS, 0, -1):
        children = 2 ** level
        child_size = devices_all // children
        right_rows = right_basis[level - 1].reshape(devices_all, LEAF, RANK).astype(jnp.float32)
        partial_value = jnp.einsum("dlr,dlc->drc", right_rows, solution, precision=lax.Precision.HIGHEST)
        sums = partial_value.reshape(children, child_size, RANK, COLS).sum(axis=1)
        stacked = sums.reshape(children // 2, 2 * RANK, COLS)
        reduced = reduced_all[level - 1].reshape(children // 2, 2 * RANK, 2 * RANK)
        mixed = jnp.einsum("nij,njc->nic", reduced, stacked, precision=lax.Precision.HIGHEST)
        mixed = mixed.reshape(children, RANK, COLS)
        per_device = jnp.repeat(mixed, child_size, axis=0)
        left_rows = left_basis[level - 1].reshape(devices_all, LEAF, RANK).astype(jnp.float32)
        solution = solution - jnp.einsum("dlr,drc->dlc", left_rows, per_device, precision=lax.Precision.HIGHEST)
    return solution.reshape(devices_all * LEAF, COLS)
```

```python
import functools

import jax
import jax.numpy as jnp
from jax import lax
from jax.experimental import pallas as pl
from jax.experimental.pallas import tpu as pltpu
from jax.sharding import PartitionSpec as P

LEVELS = 4
MESH = pl.DeviceIdType.MESH
F32 = jnp.float32
BF16 = jnp.bfloat16
HIGHEST = lax.Precision.HIGHEST
PAIRS = [(j, k) for k in range(LEVELS, 0, -1) for j in range(k - 1, 0, -1)]


def halves(value):
    high = value.astype(BF16)
    return high, (value - high.astype(F32)).astype(BF16)


def flip(position, mask):
    bit, result = 1, position
    while bit <= mask:
        if mask & bit:
            result = result + bit * (1 - 2 * ((position // bit) % 2))
        bit *= 2
    return result


def plan(depth):
    plans = {}
    for level in range(LEVELS, 0, -1):
        sibling = depth - level
        scattered = 2 if sibling - 1 >= 2 else 0
        plans[level] = (sibling, scattered, list(range(1 + scattered, sibling)))
    return plans


def kernel(depth, rank, *refs):
    plans = plan(depth)
    (rhs_h, inv_h, right_h, left_h), reduced_h, out_h = refs[:4], refs[4:8], refs[8]
    it = iter(refs[9:])
    rhs, inv, right, left, x, proj, proj_in = (next(it) for _ in range(7))
    gram, gram_in, own = next(it), next(it), next(it)
    load_sem, out_sem = next(it), next(it)
    core_send, core_recv = next(it), next(it)
    per = {}
    for level in range(LEVELS, 0, -1):
        per[level] = [next(it) for _ in range(12)]
    both = {level: per[level][6] for level in per}

    me = lax.axis_index("leaf")
    core = me % 2
    partner = flip(me, 1)
    leaf, cols = x.shape
    wide = cols // 2

    loads = [
        pltpu.make_async_copy(rhs_h, rhs, load_sem.at[0]),
        pltpu.make_async_copy(inv_h, inv, load_sem.at[1]),
    ]
    for level in range(LEVELS, 0, -1):
        loads.append(pltpu.make_async_copy(right_h.at[level - 1], right.at[level - 1], load_sem.at[2 * level]))
        loads.append(pltpu.make_async_copy(left_h.at[level - 1], left.at[level - 1], load_sem.at[2 * level + 1]))
    base = 2 + 2 * LEVELS
    for level in range(LEVELS, 0, -1):
        loads.append(
            pltpu.make_async_copy(reduced_h[level - 1], per[level][0].at[core], load_sem.at[base + level - 1])
        )
    for copy in loads:
        copy.start()
    right_load = {LEVELS - i: loads[2 + 2 * i] for i in range(LEVELS)}
    left_load = {LEVELS - i: loads[3 + 2 * i] for i in range(LEVELS)}
    reduced_load = {LEVELS - i: loads[base + i] for i in range(LEVELS)}

    top = plans[1][0]
    masks = [1] + [q * 2 for q in range(1, 1 << (top - 1))] + [1 << top]
    barrier = pltpu.get_barrier_semaphore()
    for mask in masks:
        pl.semaphore_signal(barrier, inc=1, device_id=(flip(me, mask),), device_id_type=MESH)

    pending = []

    def send(src, dst, send_sem, recv_sem, target):
        copy = pltpu.make_async_remote_copy(
            src_ref=src, dst_ref=dst, send_sem=send_sem, recv_sem=recv_sem, device_id=(target,), device_id_type=MESH
        )
        copy.start()
        pending.append(copy)
        return copy

    core_count = [0]

    def core_send_to(src, dst):
        i = core_count[0]
        core_count[0] += 1
        return send(src, dst, core_send.at[i], core_recv.at[i], partner)

    loads[0].wait()
    loads[1].wait()
    tile = leaf // 4

    def leaf_step(i, carry):
        rows = pl.ds(pl.multiple_of(i * tile, tile), tile)
        x[rows, :] = jnp.dot(inv[rows, :], rhs[...], preferred_element_type=F32)
        return carry

    lax.fori_loop(0, leaf // tile, leaf_step, 0)
    x_high, x_low = halves(x[...])

    def tdot(a, b):
        return lax.dot_general(a, b, (((0,), (0,)), ((), ())), preferred_element_type=F32)

    proj_copy, gram_copy, reduced_copy, both_copy = {}, {}, {}, {}

    def project(level):
        right_load[level].wait()
        basis = right[level - 1]
        value = tdot(basis, x_high) + tdot(basis, x_low)
        proj[level - 1, 0] = value[:, :wide]
        proj[level - 1, 1] = value[:, wide:]

    def project_send(level):
        proj_copy[level] = core_send_to(proj.at[level - 1, 1 - core], proj_in.at[level - 1])

    def reduced_send(level):
        reduced_load[level].wait()
        kbuf = per[level][0]
        reduced_copy[level] = core_send_to(kbuf.at[core], kbuf.at[core])

    project(LEVELS)
    pl.semaphore_wait(barrier, len(masks))
    project_send(LEVELS)
    reduced_send(LEVELS)

    def prepare():
        for level in range(LEVELS - 1, 0, -1):
            project(level)
            project_send(level)
            for k in range(LEVELS, level, -1):
                if level == LEVELS - 1:
                    left_load[k].wait()
                elif k == level + 1:
                    left_load[k].wait()
                index = PAIRS.index((level, k))
                gram[index] = tdot(right[level - 1], left[k - 1])
                gram_copy[level, k] = core_send_to(gram.at[index], gram_in.at[index])
            reduced_send(level)
        left_load[1].wait()

    def take_proj(level):
        proj_copy[level].wait_recv()
        own[level - 1] = proj[level - 1, core] + proj_in[level - 1]

    def take_gram(level, k):
        gram_copy[level, k].wait_recv()
        index = PAIRS.index((level, k))
        gram_in[index] = gram[index] + gram_in[index]

    def eliminate(level, k):
        index = PAIRS.index((level, k))
        own[level - 1] -= jnp.dot(
            gram_in[index], both[k][core], precision=HIGHEST, preferred_element_type=F32
        )

    def apply(k):
        both_copy[k].wait_recv()
        pieces = [halves(both[k][side]) for side in range(2)]
        high = jnp.concatenate([piece[0] for piece in pieces], 1)
        low = jnp.concatenate([piece[1] for piece in pieces], 1)

        def step(i, carry):
            rows = pl.ds(pl.multiple_of(i * tile, tile), tile)
            w = left[k - 1, rows, :]
            x[rows, :] -= jnp.dot(w, high, preferred_element_type=F32) + jnp.dot(w, low, preferred_element_type=F32)
            return carry

        lax.fori_loop(0, leaf // tile, step, 0)

    def level_step(level, aside):
        kbuf, scatter_in, chain, chain_in, stk, slabs, full = per[level][:7]
        s_send, s_recv, c_sem, g_sem, m_sem = per[level][7:]
        sibling, scattered, butterfly = plans[level]
        parts = 1 << scattered
        size = rank // parts
        place = (me // 2) % parts
        mine = pl.ds(pl.multiple_of(place * size, size), size)
        upper = (me // (1 << sibling)) % 2
        aside = list(aside)

        def beside():
            if aside:
                aside.pop(0)()

        if scattered:
            copies = []
            for q in range(1, parts):
                peer_place = flip(place, q)
                rows = pl.ds(pl.multiple_of(peer_place * size, size), size)
                copies.append(
                    send(own.at[level - 1, rows], scatter_in.at[q], s_send.at[q], s_recv.at[q], flip(me, 2 * q))
                )
            beside()
            total = own[level - 1, mine, :]
            for q, copy in enumerate(copies, 1):
                copy.wait_recv()
                total = total + scatter_in[q]
        else:
            total = own[level - 1]
        for i, bit in enumerate(butterfly):
            chain[i] = total
            copy = send(chain.at[i], chain_in.at[i], c_sem.at[0, i], c_sem.at[1, i], flip(me, 1 << bit))
            beside()
            copy.wait_recv()
            total = total + chain_in[i]
        stk[upper, mine, :] = total
        here = stk.at[upper, mine]
        cross = send(here, here, g_sem.at[0, 0, 0], g_sem.at[1, 0, 0], flip(me, 1 << sibling))
        gathers = []
        for q in range(1, parts):
            gathers.append(send(here, here, g_sem.at[0, 0, q], g_sem.at[1, 0, q], flip(me, 2 * q)))
        beside()
        cross.wait_recv()
        there = stk.at[1 - upper, mine]
        for q in range(1, parts):
            gathers.append(send(there, there, g_sem.at[0, 1, q], g_sem.at[1, 1, q], flip(me, 2 * q)))
        beside()
        reduced_copy[level].wait_recv()
        rows = kbuf.shape[1] * 2
        chip_rows = kbuf[...].reshape(rows, 2 * rank)
        for copy in gathers:
            copy.wait_recv()
        mixed = jnp.dot(
            chip_rows, stk[...].reshape(2 * rank, wide), precision=HIGHEST, preferred_element_type=F32
        )
        chips = 1 << (sibling - 1)
        if chips == 1:
            full[core] = mixed
        else:
            slot = (me // 2) % chips
            slabs[slot] = mixed
            spread = [
                send(slabs.at[slot], slabs.at[slot], m_sem.at[0, q], m_sem.at[1, q], flip(me, 2 * q))
                for q in range(1, chips)
            ]
            while aside:
                beside()
            for copy in spread:
                copy.wait_recv()
            full[core] = slabs[...].reshape(rank, wide)
        while aside:
            beside()
        both_copy[level] = core_send_to(full.at[core], full.at[core])

    take_proj(LEVELS)
    level_step(LEVELS, [prepare])
    for level in range(LEVELS - 1, 0, -1):
        k = level + 1
        if k == LEVELS:
            take_proj(level)
            take_gram(level, k)
        eliminate(level, k)

        def rest(k=k):
            if k == LEVELS:
                for j in range(LEVELS - 2, 0, -1):
                    take_proj(j)
                for j, other in PAIRS:
                    if (j, other) != (LEVELS - 1, LEVELS):
                        take_gram(j, other)
            for j in range(k - 2, 0, -1):
                eliminate(j, k)

        level_step(level, [rest, functools.partial(apply, k)])
    apply(1)
    store = pltpu.make_async_copy(x, out_h, out_sem)
    store.start()
    for copy in pending:
        copy.wait_send()
    store.wait()


def local(right_side, leaf_inv, right_basis, left_basis, *reduced):
    devices = lax.axis_size("leaf")
    depth = devices.bit_length() - 1
    leaf, cols = right_side.shape
    rank = right_basis.shape[2]
    wide = cols // 2
    scratch = [
        pltpu.VMEM(right_side.shape, BF16),
        pltpu.VMEM(leaf_inv.shape, BF16),
        pltpu.VMEM(right_basis.shape, BF16),
        pltpu.VMEM(left_basis.shape, BF16),
        pltpu.VMEM((leaf, cols), F32),
        pltpu.VMEM((LEVELS, 2, rank, wide), F32),
        pltpu.VMEM((LEVELS, rank, wide), F32),
        pltpu.VMEM((len(PAIRS), rank, rank), F32),
        pltpu.VMEM((len(PAIRS), rank, rank), F32),
        pltpu.VMEM((LEVELS, rank, wide), F32),
        pltpu.SemaphoreType.DMA((2 + 3 * LEVELS,)),
        pltpu.SemaphoreType.DMA,
        pltpu.SemaphoreType.DMA((3 * LEVELS + len(PAIRS),)),
        pltpu.SemaphoreType.DMA((3 * LEVELS + len(PAIRS),)),
    ]
    plans = plan(depth)
    for level in range(LEVELS, 0, -1):
        sibling, scattered, butterfly = plans[level]
        parts = 1 << scattered
        steps = max(1, len(butterfly))
        chips = 1 << (sibling - 1)
        rows = reduced[level - 1].shape[0]
        scratch += [
            pltpu.VMEM((2, rows, 2 * rank), F32),
            pltpu.VMEM((parts, rank // parts, wide), F32),
            pltpu.VMEM((steps, rank // parts, wide), F32),
            pltpu.VMEM((steps, rank // parts, wide), F32),
            pltpu.VMEM((2, rank, wide), F32),
            pltpu.VMEM((chips, 2 * rows, wide), F32),
            pltpu.VMEM((2, rank, wide), F32),
            pltpu.SemaphoreType.DMA((parts,)),
            pltpu.SemaphoreType.DMA((parts,)),
            pltpu.SemaphoreType.DMA((2, steps)),
            pltpu.SemaphoreType.DMA((2, 2, parts)),
            pltpu.SemaphoreType.DMA((2, chips)),
        ]
    return pl.pallas_call(
        functools.partial(kernel, depth, rank),
        out_shape=jax.ShapeDtypeStruct((leaf, cols), F32),
        in_specs=[pl.BlockSpec(memory_space=pl.ANY)] * (4 + LEVELS),
        out_specs=pl.BlockSpec(memory_space=pl.ANY),
        scratch_shapes=scratch,
        compiler_params=pltpu.CompilerParams(
            collective_id=0, has_side_effects=True, vmem_limit_bytes=40 * 1024 * 1024
        ),
        name="tree_solve",
    )(right_side, leaf_inv, right_basis, left_basis, *reduced)


def solution(mesh):
    return jax.shard_map(
        local,
        mesh=mesh,
        in_specs=(
            P("leaf", None),
            P("leaf", None),
            P(None, "leaf", None),
            P(None, "leaf", None),
            P("leaf", None),
            P("leaf", None),
            P("leaf", None),
            P("leaf", None),
        ),
        out_specs=P("leaf", None),
        check_vma=False,
    )
```

```python
import functools

import jax
import jax.numpy as jnp
from jax import lax
from jax.experimental import pallas as pl
from jax.experimental.pallas import tpu as pltpu
from jax.sharding import PartitionSpec as P

LEVELS = 4
TILES = 4
MESH = pl.DeviceIdType.MESH
F32 = jnp.float32
BF16 = jnp.bfloat16
HIGHEST = lax.Precision.HIGHEST
PAIRS = [(j, k) for k in range(LEVELS, 0, -1) for j in range(k - 1, 0, -1)]


def halves(value):
    high = value.astype(BF16)
    return high, (value - high.astype(F32)).astype(BF16)


def flip(position, mask):
    bit, result = 1, position
    while bit <= mask:
        if mask & bit:
            result = result + bit * (1 - 2 * ((position // bit) % 2))
        bit *= 2
    return result


def plan(depth):
    plans = {}
    for level in range(LEVELS, 0, -1):
        sibling = depth - level
        scattered = 2 if sibling - 1 >= 2 else 0
        plans[level] = (sibling, scattered, list(range(1 + scattered, sibling)))
    return plans


def kernel(depth, rank, *refs):
    plans = plan(depth)
    (rhs_h, inv_h, right_h, left_h), reduced_h, out_h = refs[:4], refs[4:8], refs[8]
    it = iter(refs[9:])
    rhs, inv, right, left, x, proj, proj_in = (next(it) for _ in range(7))
    gram, gram_in, own = next(it), next(it), next(it)
    load_sem, out_sem = next(it), next(it)
    core_send, core_recv = next(it), next(it)
    per = {}
    for level in range(LEVELS, 0, -1):
        per[level] = [next(it) for _ in range(11)]
    both = {level: per[level][5] for level in per}

    me = lax.axis_index("leaf")
    core = me % 2
    partner = flip(me, 1)
    leaf, cols = x.shape
    wide = cols // 2

    tile = leaf // TILES
    slots = {level: (me // 2) % (1 << (plans[level][0] - 1)) for level in plans}
    loads = [pltpu.make_async_copy(rhs_h, rhs, load_sem.at[0])]
    for i in range(TILES):
        rows = pl.ds(i * tile, tile)
        loads.append(pltpu.make_async_copy(inv_h.at[rows], inv.at[rows], load_sem.at[2 + 3 * LEVELS + i]))
    inv_load = loads[1:]
    first = len(loads)
    for level in range(LEVELS, 0, -1):
        loads.append(pltpu.make_async_copy(right_h.at[level - 1], right.at[level - 1], load_sem.at[2 * level]))
        loads.append(pltpu.make_async_copy(left_h.at[level - 1], left.at[level - 1], load_sem.at[2 * level + 1]))
    base = 2 + 2 * LEVELS
    for level in range(LEVELS, 0, -1):
        loads.append(
            pltpu.make_async_copy(
                reduced_h[level - 1], per[level][0].at[slots[level], core], load_sem.at[base + level - 1]
            )
        )
    right_load = {LEVELS - i: loads[first + 2 * i] for i in range(LEVELS)}
    left_load = {LEVELS - i: loads[first + 1 + 2 * i] for i in range(LEVELS)}
    reduced_load = {LEVELS - i: loads[first + 2 * LEVELS + i] for i in range(LEVELS)}
    early = list(reduced_load.values()) + loads[:first] + [right_load[LEVELS]]
    for copy in early:
        copy.start()

    top = plans[1][0]
    masks = [1] + [q * 2 for q in range(1, 1 << (top - 1))] + [1 << top]
    barrier = pltpu.get_barrier_semaphore()
    for mask in masks:
        pl.semaphore_signal(barrier, inc=1, device_id=(flip(me, mask),), device_id_type=MESH)

    pending = []

    def send(src, dst, send_sem, recv_sem, target):
        copy = pltpu.make_async_remote_copy(
            src_ref=src, dst_ref=dst, send_sem=send_sem, recv_sem=recv_sem, device_id=(target,), device_id_type=MESH
        )
        copy.start()
        pending.append(copy)
        return copy

    core_count = [0]

    def core_send_to(src, dst):
        i = core_count[0]
        core_count[0] += 1
        return send(src, dst, core_send.at[i], core_recv.at[i], partner)

    spread = {}

    def reduced_spread(level):
        reduced_load[level].wait()
        kbuf, k_sem = per[level][0], per[level][-1]
        piece = kbuf.at[slots[level], core]
        spread[level] = [
            send(piece, piece, k_sem.at[0, q], k_sem.at[1, q], flip(me, 2 * q)) for q in range(1, kbuf.shape[0])
        ]
        spread[level].insert(0, send(piece, piece, k_sem.at[2, 0], k_sem.at[3, 0], partner))

    def reduced_forward(level):
        kbuf, k_sem = per[level][0], per[level][-1]
        reduced_copy[level] = [spread[level][0]]
        for q in range(1, kbuf.shape[0]):
            spread[level][q].wait_recv()
            piece = kbuf.at[flip(slots[level], q), core]
            reduced_copy[level].append(send(piece, piece, k_sem.at[2, q], k_sem.at[3, q], partner))

    pl.semaphore_wait(barrier, len(masks))
    for level in range(LEVELS, 1, -1):
        reduced_spread(level)

    loads[0].wait()
    for i in range(TILES):
        inv_load[i].wait()
        if i == 0:
            for copy in loads:
                if all(copy is not other for other in early):
                    copy.start()
        rows = pl.ds(i * tile, tile)
        x[rows, :] = jnp.dot(inv[rows, :], rhs[...], preferred_element_type=F32)
    x_high, x_low = halves(x[...])

    def tdot(a, b):
        return lax.dot_general(a, b, (((0,), (0,)), ((), ())), preferred_element_type=F32)

    proj_copy, gram_copy, reduced_copy, both_copy = {}, {}, {}, {}

    def project(level):
        right_load[level].wait()
        basis = right[level - 1]
        value = tdot(basis, x_high) + tdot(basis, x_low)
        proj[level - 1, 0] = value[:, :wide]
        proj[level - 1, 1] = value[:, wide:]

    def project_send(level):
        proj_copy[level] = core_send_to(proj.at[level - 1, 1 - core], proj_in.at[level - 1])

    project(LEVELS)
    project_send(LEVELS)
    reduced_forward(LEVELS)

    def prepare():
        for level in range(LEVELS - 1, 0, -1):
            project(level)
            project_send(level)
            for k in range(LEVELS, level, -1):
                if level == LEVELS - 1:
                    left_load[k].wait()
                elif k == level + 1:
                    left_load[k].wait()
                index = PAIRS.index((level, k))
                gram[index] = tdot(right[level - 1], left[k - 1])
                gram_copy[level, k] = core_send_to(gram.at[index], gram_in.at[index])
            if level == LEVELS - 1:
                reduced_forward(level)
        left_load[1].wait()

    def take_proj(level):
        proj_copy[level].wait_recv()
        own[level - 1] = proj[level - 1, core] + proj_in[level - 1]

    def take_gram(level, k):
        gram_copy[level, k].wait_recv()
        index = PAIRS.index((level, k))
        gram_in[index] = gram[index] + gram_in[index]

    def eliminate(level, k):
        index = PAIRS.index((level, k))
        own[level - 1] -= jnp.dot(
            gram_in[index], both[k][core], precision=HIGHEST, preferred_element_type=F32
        )

    def apply(k):
        both_copy[k].wait_recv()
        pieces = [halves(both[k][side]) for side in range(2)]
        high = jnp.concatenate([piece[0] for piece in pieces], 1)
        low = jnp.concatenate([piece[1] for piece in pieces], 1)

        def step(i, carry):
            rows = pl.ds(pl.multiple_of(i * tile, tile), tile)
            w = left[k - 1, rows, :]
            x[rows, :] -= jnp.dot(w, high, preferred_element_type=F32) + jnp.dot(w, low, preferred_element_type=F32)
            return carry

        lax.fori_loop(0, leaf // tile, step, 0)

    def level_step(level, aside):
        kbuf, scatter_in, chain, chain_in, stk, full = per[level][:6]
        s_send, s_recv, c_sem, g_sem = per[level][6:10]
        sibling, scattered, butterfly = plans[level]
        parts = 1 << scattered
        size = rank // parts
        place = (me // 2) % parts
        mine = pl.ds(pl.multiple_of(place * size, size), size)
        upper = (me // (1 << sibling)) % 2
        aside = list(aside)

        def beside():
            if aside:
                aside.pop(0)()

        if scattered:
            copies = []
            for q in range(1, parts):
                peer_place = flip(place, q)
                rows = pl.ds(pl.multiple_of(peer_place * size, size), size)
                copies.append(
                    send(own.at[level - 1, rows], scatter_in.at[q], s_send.at[q], s_recv.at[q], flip(me, 2 * q))
                )
            beside()
            total = own[level - 1, mine, :]
            for q, copy in enumerate(copies, 1):
                copy.wait_recv()
                total = total + scatter_in[q]
        else:
            total = own[level - 1]
        gathers, crosses = [], []
        sister = flip(me, 1 << sibling)
        if not scattered and butterfly:
            piece = rank // TILES
            chunks = [pl.ds(i * piece, piece) for i in range(TILES)]
            sums = [
                send(
                    own.at[level - 1, rows],
                    chain_in.at[0, rows],
                    c_sem.at[0, i],
                    c_sem.at[1, i],
                    flip(me, 1 << butterfly[0]),
                )
                for i, rows in enumerate(chunks)
            ]
            beside()
            for i, rows in enumerate(chunks):
                sums[i].wait_recv()
                stk[upper, rows, :] = own[level - 1, rows, :] + chain_in[0, rows, :]
                here = stk.at[upper, rows]
                crosses.append(send(here, here, g_sem.at[0, 0, i], g_sem.at[1, 0, i], sister))
        else:
            for i, bit in enumerate(butterfly):
                chain[i] = total
                copy = send(chain.at[i], chain_in.at[i], c_sem.at[0, i], c_sem.at[1, i], flip(me, 1 << bit))
                beside()
                copy.wait_recv()
                total = total + chain_in[i]
            stk[upper, mine, :] = total
            here = stk.at[upper, mine]
            crosses.append(send(here, here, g_sem.at[0, 0, 0], g_sem.at[1, 0, 0], sister))
            for q in range(1, parts):
                gathers.append(send(here, here, g_sem.at[0, 0, q], g_sem.at[1, 0, q], flip(me, 2 * q)))
        beside()
        for copy in crosses:
            copy.wait_recv()
        there = stk.at[1 - upper, mine]
        for q in range(1, parts):
            gathers.append(send(there, there, g_sem.at[0, 1, q], g_sem.at[1, 1, q], flip(me, 2 * q)))
        while aside:
            beside()
        for copy in reduced_copy[level]:
            copy.wait_recv()
        for copy in gathers:
            copy.wait_recv()
        full[core] = jnp.dot(
            kbuf[...].reshape(rank, 2 * rank),
            stk[...].reshape(2 * rank, wide),
            precision=HIGHEST,
            preferred_element_type=F32,
        )
        both_copy[level] = core_send_to(full.at[core], full.at[core])

    take_proj(LEVELS)
    level_step(LEVELS, [prepare])
    for level in range(LEVELS - 1, 0, -1):
        k = level + 1
        if k == LEVELS:
            take_proj(level)
            take_gram(level, k)
        eliminate(level, k)

        def rest(k=k, level=level):
            if k == LEVELS:
                for j in range(LEVELS - 2, 0, -1):
                    take_proj(j)
                for j, other in PAIRS:
                    if (j, other) != (LEVELS - 1, LEVELS):
                        take_gram(j, other)
            if level == 2:
                reduced_spread(1)
            if k == LEVELS:
                reduced_forward(2)

        def tail(k=k):
            for j in range(k - 2, 0, -1):
                eliminate(j, k)
            if k == 2:
                reduced_forward(1)
            apply(k)

        level_step(level, [rest, tail])
    apply(1)
    store = pltpu.make_async_copy(x, out_h, out_sem)
    store.start()
    for copy in pending:
        copy.wait_send()
    store.wait()


def local(right_side, leaf_inv, right_basis, left_basis, *reduced):
    devices = lax.axis_size("leaf")
    depth = devices.bit_length() - 1
    leaf, cols = right_side.shape
    rank = right_basis.shape[2]
    wide = cols // 2
    scratch = [
        pltpu.VMEM(right_side.shape, BF16),
        pltpu.VMEM(leaf_inv.shape, BF16),
        pltpu.VMEM(right_basis.shape, BF16),
        pltpu.VMEM(left_basis.shape, BF16),
        pltpu.VMEM((leaf, cols), F32),
        pltpu.VMEM((LEVELS, 2, rank, wide), F32),
        pltpu.VMEM((LEVELS, rank, wide), F32),
        pltpu.VMEM((len(PAIRS), rank, rank), F32),
        pltpu.VMEM((len(PAIRS), rank, rank), F32),
        pltpu.VMEM((LEVELS, rank, wide), F32),
        pltpu.SemaphoreType.DMA((2 + 3 * LEVELS + TILES,)),
        pltpu.SemaphoreType.DMA,
        pltpu.SemaphoreType.DMA((2 * LEVELS + len(PAIRS),)),
        pltpu.SemaphoreType.DMA((2 * LEVELS + len(PAIRS),)),
    ]
    plans = plan(depth)
    for level in range(LEVELS, 0, -1):
        sibling, scattered, butterfly = plans[level]
        parts = 1 << scattered
        steps = max(1, len(butterfly))
        chips = 1 << (sibling - 1)
        rows = reduced[level - 1].shape[0]
        scratch += [
            pltpu.VMEM((chips, 2, rows, 2 * rank), F32),
            pltpu.VMEM((parts, rank // parts, wide), F32),
            pltpu.VMEM((steps, rank // parts, wide), F32),
            pltpu.VMEM((steps, rank // parts, wide), F32),
            pltpu.VMEM((2, rank, wide), F32),
            pltpu.VMEM((2, rank, wide), F32),
            pltpu.SemaphoreType.DMA((parts,)),
            pltpu.SemaphoreType.DMA((parts,)),
            pltpu.SemaphoreType.DMA((2, max(steps, TILES))),
            pltpu.SemaphoreType.DMA((2, 2, max(parts, TILES))),
            pltpu.SemaphoreType.DMA((4, chips)),
        ]
    return pl.pallas_call(
        functools.partial(kernel, depth, rank),
        out_shape=jax.ShapeDtypeStruct((leaf, cols), F32),
        in_specs=[pl.BlockSpec(memory_space=pltpu.HBM)] * (4 + LEVELS),
        out_specs=pl.BlockSpec(memory_space=pl.ANY),
        scratch_shapes=scratch,
        compiler_params=pltpu.CompilerParams(
            collective_id=0, has_side_effects=True, vmem_limit_bytes=56 * 1024 * 1024
        ),
        name="tree_solve",
    )(right_side, leaf_inv, right_basis, left_basis, *reduced)


def solution(mesh):
    return jax.shard_map(
        local,
        mesh=mesh,
        in_specs=(
            P("leaf", None),
            P("leaf", None),
            P(None, "leaf", None),
            P(None, "leaf", None),
            P("leaf", None),
            P("leaf", None),
            P("leaf", None),
            P("leaf", None),
        ),
        out_specs=P("leaf", None),
        check_vma=False,
    )
```

```python
import functools

import jax
import jax.numpy as jnp
from jax import lax
from jax.experimental import pallas as pl
from jax.experimental.pallas import tpu as pltpu
from jax.sharding import PartitionSpec as P

LEVELS = 4
TILES = 4
MESH = pl.DeviceIdType.MESH
F32 = jnp.float32
BF16 = jnp.bfloat16
PAIRS = [(j, k) for k in range(LEVELS, 0, -1) for j in range(k - 1, 0, -1)]


def halves(value):
    high = value.astype(BF16)
    return high, (value - high.astype(F32)).astype(BF16)


def split_dot(left_parts, value):
    (high, low), (top, rest) = left_parts, halves(value)
    wide = value.shape[1]
    both = jnp.dot(high, jnp.concatenate([top, rest], 1), preferred_element_type=F32)
    return both[:, :wide] + both[:, wide:] + jnp.dot(low, top, preferred_element_type=F32)


def flip(position, mask):
    bit, result = 1, position
    while bit <= mask:
        if mask & bit:
            result = result + bit * (1 - 2 * ((position // bit) % 2))
        bit *= 2
    return result


def plan(depth):
    plans = {}
    for level in range(LEVELS, 0, -1):
        sibling = depth - level
        scattered = 2 if sibling - 1 >= 2 else 0
        plans[level] = (sibling, scattered, list(range(1 + scattered, sibling)))
    return plans


def kernel(depth, rank, *refs):
    plans = plan(depth)
    (rhs_h, inv_h, right_h, left_h), reduced_h, out_h = refs[:4], refs[4:8], refs[8]
    it = iter(refs[9:])
    rhs, inv, right, left, x, proj, proj_in = (next(it) for _ in range(7))
    gram, gram_in, own = next(it), next(it), next(it)
    load_sem, out_sem = next(it), next(it)
    core_send, core_recv = next(it), next(it)
    per = {}
    for level in range(LEVELS, 0, -1):
        per[level] = [next(it) for _ in range(11)]
    both = {level: per[level][5] for level in per}

    me = lax.axis_index("leaf")
    core = me % 2
    partner = flip(me, 1)
    leaf, cols = x.shape
    wide = cols // 2

    tile = leaf // TILES
    slots = {level: (me // 2) % (1 << (plans[level][0] - 1)) for level in plans}
    loads = [pltpu.make_async_copy(rhs_h, rhs, load_sem.at[0])]
    for i in range(TILES):
        rows = pl.ds(i * tile, tile)
        loads.append(pltpu.make_async_copy(inv_h.at[rows], inv.at[rows], load_sem.at[2 + 3 * LEVELS + i]))
    inv_load = loads[1:]
    first = len(loads)
    for level in range(LEVELS, 0, -1):
        loads.append(pltpu.make_async_copy(right_h.at[level - 1], right.at[level - 1], load_sem.at[2 * level]))
        loads.append(pltpu.make_async_copy(left_h.at[level - 1], left.at[level - 1], load_sem.at[2 * level + 1]))
    base = 2 + 2 * LEVELS
    for level in range(LEVELS, 0, -1):
        loads.append(
            pltpu.make_async_copy(
                reduced_h[level - 1], per[level][0].at[slots[level], core], load_sem.at[base + level - 1]
            )
        )
    right_load = {LEVELS - i: loads[first + 2 * i] for i in range(LEVELS)}
    left_load = {LEVELS - i: loads[first + 1 + 2 * i] for i in range(LEVELS)}
    reduced_load = {LEVELS - i: loads[first + 2 * LEVELS + i] for i in range(LEVELS)}
    early = list(reduced_load.values()) + loads[:first] + [right_load[LEVELS]]
    for copy in early:
        copy.start()

    top = plans[1][0]
    masks = [1] + [q * 2 for q in range(1, 1 << (top - 1))] + [1 << top]
    barrier = pltpu.get_barrier_semaphore()
    for mask in masks:
        pl.semaphore_signal(barrier, inc=1, device_id=(flip(me, mask),), device_id_type=MESH)

    pending = []

    def send(src, dst, send_sem, recv_sem, target):
        copy = pltpu.make_async_remote_copy(
            src_ref=src, dst_ref=dst, send_sem=send_sem, recv_sem=recv_sem, device_id=(target,), device_id_type=MESH
        )
        copy.start()
        pending.append(copy)
        return copy

    core_count = [0]

    def core_send_to(src, dst):
        i = core_count[0]
        core_count[0] += 1
        return send(src, dst, core_send.at[i], core_recv.at[i], partner)

    spread = {}

    def reduced_spread(level):
        reduced_load[level].wait()
        kbuf, k_sem = per[level][0], per[level][-1]
        piece = kbuf.at[slots[level], core]
        spread[level] = [
            send(piece, piece, k_sem.at[0, q], k_sem.at[1, q], flip(me, 2 * q)) for q in range(1, kbuf.shape[0])
        ]
        spread[level].insert(0, send(piece, piece, k_sem.at[2, 0], k_sem.at[3, 0], partner))

    def reduced_forward(level):
        kbuf, k_sem = per[level][0], per[level][-1]
        reduced_copy[level] = [spread[level][0]]
        for q in range(1, kbuf.shape[0]):
            spread[level][q].wait_recv()
            piece = kbuf.at[flip(slots[level], q), core]
            reduced_copy[level].append(send(piece, piece, k_sem.at[2, q], k_sem.at[3, q], partner))

    pl.semaphore_wait(barrier, len(masks))
    for level in range(LEVELS, 1, -1):
        reduced_spread(level)

    loads[0].wait()
    for i in range(TILES):
        inv_load[i].wait()
        if i == 0:
            for copy in loads:
                if all(copy is not other for other in early):
                    copy.start()
        rows = pl.ds(i * tile, tile)
        x[rows, :] = jnp.dot(inv[rows, :], rhs[...], preferred_element_type=F32)
    x_high, x_low = halves(x[...])

    def tdot(a, b):
        return lax.dot_general(a, b, (((0,), (0,)), ((), ())), preferred_element_type=F32)

    proj_copy, gram_copy, reduced_copy, both_copy = {}, {}, {}, {}

    def project(level):
        right_load[level].wait()
        basis = right[level - 1]
        value = tdot(basis, x_high) + tdot(basis, x_low)
        proj[level - 1, 0] = value[:, :wide]
        proj[level - 1, 1] = value[:, wide:]

    def project_send(level):
        proj_copy[level] = core_send_to(proj.at[level - 1, 1 - core], proj_in.at[level - 1])

    project(LEVELS)
    project_send(LEVELS)
    reduced_forward(LEVELS)

    def prepare():
        for level in range(LEVELS - 1, 0, -1):
            project(level)
            project_send(level)
            for k in range(LEVELS, level, -1):
                if level == LEVELS - 1:
                    left_load[k].wait()
                elif k == level + 1:
                    left_load[k].wait()
                index = PAIRS.index((level, k))
                gram[index] = tdot(right[level - 1], left[k - 1])
                gram_copy[level, k] = core_send_to(gram.at[index], gram_in.at[index])
            if level == LEVELS - 1:
                reduced_forward(level)
        left_load[1].wait()

    def take_proj(level):
        proj_copy[level].wait_recv()
        own[level - 1] = proj[level - 1, core] + proj_in[level - 1]

    def take_gram(level, k):
        gram_copy[level, k].wait_recv()
        index = PAIRS.index((level, k))
        gram_in[index] = gram[index] + gram_in[index]

    def eliminate(level, k):
        index = PAIRS.index((level, k))
        own[level - 1] -= split_dot(halves(gram_in[index]), both[k][core])

    stores = []

    def apply(k, last=False):
        both_copy[k].wait_recv()
        pieces = [halves(both[k][side]) for side in range(2)]
        high = jnp.concatenate([piece[0] for piece in pieces], 1)
        low = jnp.concatenate([piece[1] for piece in pieces], 1)

        for i in range(TILES):
            rows = pl.ds(i * tile, tile)
            w = left[k - 1, rows, :]
            x[rows, :] -= jnp.dot(w, high, preferred_element_type=F32) + jnp.dot(w, low, preferred_element_type=F32)
            if last:
                stores.append(pltpu.make_async_copy(x.at[rows], out_h.at[rows], out_sem.at[i]))
                stores[-1].start()

    def level_step(level, aside):
        kbuf, scatter_in, chain, chain_in, stk, full = per[level][:6]
        s_send, s_recv, c_sem, g_sem = per[level][6:10]
        sibling, scattered, butterfly = plans[level]
        parts = 1 << scattered
        size = rank // parts
        place = (me // 2) % parts
        mine = pl.ds(pl.multiple_of(place * size, size), size)
        upper = (me // (1 << sibling)) % 2
        aside = list(aside)

        def beside():
            if aside:
                aside.pop(0)()

        if scattered:
            copies = []
            for q in range(1, parts):
                peer_place = flip(place, q)
                rows = pl.ds(pl.multiple_of(peer_place * size, size), size)
                copies.append(
                    send(own.at[level - 1, rows], scatter_in.at[q], s_send.at[q], s_recv.at[q], flip(me, 2 * q))
                )
            beside()
            total = own[level - 1, mine, :]
            for q, copy in enumerate(copies, 1):
                copy.wait_recv()
                total = total + scatter_in[q]
        else:
            total = own[level - 1]
        gathers, crosses = [], []
        sister = flip(me, 1 << sibling)
        if not scattered and butterfly:
            piece = rank // TILES
            chunks = [pl.ds(i * piece, piece) for i in range(TILES)]
            sums = [
                send(
                    own.at[level - 1, rows],
                    chain_in.at[0, rows],
                    c_sem.at[0, i],
                    c_sem.at[1, i],
                    flip(me, 1 << butterfly[0]),
                )
                for i, rows in enumerate(chunks)
            ]
            beside()
            for i, rows in enumerate(chunks):
                sums[i].wait_recv()
                stk[upper, rows, :] = own[level - 1, rows, :] + chain_in[0, rows, :]
                here = stk.at[upper, rows]
                crosses.append(send(here, here, g_sem.at[0, 0, i], g_sem.at[1, 0, i], sister))
        else:
            for i, bit in enumerate(butterfly):
                chain[i] = total
                copy = send(chain.at[i], chain_in.at[i], c_sem.at[0, i], c_sem.at[1, i], flip(me, 1 << bit))
                beside()
                copy.wait_recv()
                total = total + chain_in[i]
            stk[upper, mine, :] = total
            here = stk.at[upper, mine]
            crosses.append(send(here, here, g_sem.at[0, 0, 0], g_sem.at[1, 0, 0], sister))
            for q in range(1, parts):
                gathers.append(send(here, here, g_sem.at[0, 0, q], g_sem.at[1, 0, q], flip(me, 2 * q)))
        beside()
        for copy in crosses:
            copy.wait_recv()
        there = stk.at[1 - upper, mine]
        for q in range(1, parts):
            gathers.append(send(there, there, g_sem.at[0, 1, q], g_sem.at[1, 1, q], flip(me, 2 * q)))
        while aside:
            beside()
        for copy in reduced_copy[level]:
            copy.wait_recv()
        reduced_parts = halves(kbuf[...].reshape(rank, 2 * rank))
        for copy in gathers:
            copy.wait_recv()
        full[core] = split_dot(reduced_parts, stk[...].reshape(2 * rank, wide))
        both_copy[level] = core_send_to(full.at[core], full.at[core])

    take_proj(LEVELS)
    level_step(LEVELS, [prepare])
    for level in range(LEVELS - 1, 0, -1):
        k = level + 1
        if k == LEVELS:
            take_proj(level)
            take_gram(level, k)
        eliminate(level, k)

        def rest(level=level):
            if level == 2:
                reduced_spread(1)

        def tail(k=k):
            if k == LEVELS:
                reduced_forward(2)
            for j in range(k - 2, 0, -1):
                if k == LEVELS:
                    take_proj(j)
                    take_gram(j, k)
                eliminate(j, k)
            if k == 2:
                reduced_forward(1)
            apply(k)
            if k == LEVELS:
                for j, other in PAIRS:
                    if other < LEVELS:
                        take_gram(j, other)

        level_step(level, [rest, tail])
    apply(1, last=True)
    for copy in pending:
        copy.wait_send()
    for copy in stores:
        copy.wait()


def local(right_side, leaf_inv, right_basis, left_basis, *reduced):
    devices = lax.axis_size("leaf")
    depth = devices.bit_length() - 1
    leaf, cols = right_side.shape
    rank = right_basis.shape[2]
    wide = cols // 2
    scratch = [
        pltpu.VMEM(right_side.shape, BF16),
        pltpu.VMEM(leaf_inv.shape, BF16),
        pltpu.VMEM(right_basis.shape, BF16),
        pltpu.VMEM(left_basis.shape, BF16),
        pltpu.VMEM((leaf, cols), F32),
        pltpu.VMEM((LEVELS, 2, rank, wide), F32),
        pltpu.VMEM((LEVELS, rank, wide), F32),
        pltpu.VMEM((len(PAIRS), rank, rank), F32),
        pltpu.VMEM((len(PAIRS), rank, rank), F32),
        pltpu.VMEM((LEVELS, rank, wide), F32),
        pltpu.SemaphoreType.DMA((2 + 3 * LEVELS + TILES,)),
        pltpu.SemaphoreType.DMA((TILES,)),
        pltpu.SemaphoreType.DMA((2 * LEVELS + len(PAIRS),)),
        pltpu.SemaphoreType.DMA((2 * LEVELS + len(PAIRS),)),
    ]
    plans = plan(depth)
    for level in range(LEVELS, 0, -1):
        sibling, scattered, butterfly = plans[level]
        parts = 1 << scattered
        steps = max(1, len(butterfly))
        chips = 1 << (sibling - 1)
        rows = reduced[level - 1].shape[0]
        scratch += [
            pltpu.VMEM((chips, 2, rows, 2 * rank), F32),
            pltpu.VMEM((parts, rank // parts, wide), F32),
            pltpu.VMEM((steps, rank // parts, wide), F32),
            pltpu.VMEM((steps, rank // parts, wide), F32),
            pltpu.VMEM((2, rank, wide), F32),
            pltpu.VMEM((2, rank, wide), F32),
            pltpu.SemaphoreType.DMA((parts,)),
            pltpu.SemaphoreType.DMA((parts,)),
            pltpu.SemaphoreType.DMA((2, max(steps, TILES))),
            pltpu.SemaphoreType.DMA((2, 2, max(parts, TILES))),
            pltpu.SemaphoreType.DMA((4, chips)),
        ]
    return pl.pallas_call(
        functools.partial(kernel, depth, rank),
        out_shape=jax.ShapeDtypeStruct((leaf, cols), F32),
        in_specs=[pl.BlockSpec(memory_space=pltpu.HBM)] * (4 + LEVELS),
        out_specs=pl.BlockSpec(memory_space=pl.ANY),
        scratch_shapes=scratch,
        compiler_params=pltpu.CompilerParams(
            collective_id=0, has_side_effects=True, vmem_limit_bytes=56 * 1024 * 1024
        ),
        name="tree_solve",
    )(right_side, leaf_inv, right_basis, left_basis, *reduced)


def solution(mesh):
    return jax.shard_map(
        local,
        mesh=mesh,
        in_specs=(
            P("leaf", None),
            P("leaf", None),
            P(None, "leaf", None),
            P(None, "leaf", None),
            P("leaf", None),
            P("leaf", None),
            P("leaf", None),
            P("leaf", None),
        ),
        out_specs=P("leaf", None),
        check_vma=False,
    )
```
